512 devices in a mesh: term: 8 (over y), tensor: 64 (over z, x, core).
Axes of the slice: x: 4, y: 8, z: 8, core: 2. Of those that a mesh axis runs over, the one named last changes fastest.
Arguments:
- theta: bfloat16 [4096, 128, 128], P('tensor'), may hold values from -6 to 6
- left_env: bfloat16 [16, 256, 128, 128], P('term', 'tensor'), may hold values from -0.5 to 0.5
- right_env: bfloat16 [16, 192, 128, 128], P('term', 'tensor'), may hold values from -0.5 to 0.5
- coeff: float32 [16, 16], P('term'), may hold values from -1.8 to 1.8
- left_dims: int32 [256], P('tensor'), may hold values from 16 to 128, as said below
- right_dims: int32 [192], P('tensor'), may hold values from 16 to 128, as said below
- dest_dev: int32 [4096, 1], P('tensor'), may hold values from 0 to 63; in each aligned block of 64 rows (0 to 63, 64 to 127, ...) at most 2 rows name the same one
- right_local: int32 [4096], P('tensor'), may hold values from 0 to 2
Outputs:
- sigma: bfloat16 [4096, 128, 128], P('tensor')
The draws below stay inside these ranges and needn't reach their ends.
Inputs may be any that keep to these rules, and one draw needn't show every extreme that they name: `left_dims`: some sector has all 128 states. `right_dims`: some sector has all 128 states. `dest_dev`: at most 2 of the 64 blocks of one device name the same device.
All inputs are finite; a program needn't handle non-finite values.
Results may differ from the reference program's by a relative error of at most 0.017.
Values may be sent and summed in bfloat16 or wider, within the bound.
No kernel may reach another device: no remote copies, remote signals or barrier semaphores. Data moves between devices by JAX's collectives and lax.ppermute only.
A program may use at most 128 MiB of HBM per device.

```python
import math
import jax
import jax.numpy as jnp
import numpy as np
from jax import lax

PHYS = 16
BS = 128
RSD = 3
TPG = 2
NB = 64
NBLK = 4096
NSEC = 256
NSEC_R = 192
TERMS = 16
CAP = 2
N_TERM = 8
N_TENSOR = 64


def sector_sizes(key, count):
    values = jax.random.randint(key, (count,), BS // 8, BS + 1)
    where_full = jax.random.randint(jax.random.fold_in(key, 7), (), 0, count)
    return jnp.where(jnp.arange(count) == where_full, BS, values).astype(jnp.int32)


def draw_left_dims(key, part):
    key = jax.random.fold_in(key, 1)
    return sector_sizes(key, NSEC)


def draw_right_dims(key, part):
    key = jax.random.fold_in(key, 2)
    return sector_sizes(key, NSEC_R)


def touch_ends(drawn, stream_key, smallest, largest):
    place = [jax.random.randint(jax.random.fold_in(stream_key, axis), (), 0, length) for axis, length in enumerate(drawn.shape)]
    longest = drawn.shape.index(max(drawn.shape))
    neighbour = place[:longest] + [(place[longest] + 1) % drawn.shape[longest]] + place[longest + 1:]
    return drawn.at[tuple(place)].set(smallest).at[tuple(neighbour)].set(largest)


def block_scale(own_key, extent, shards, least, top_value):
    loudness, own = 1.0, jax.random.fold_in(own_key, 6)
    for axis_at, shards_of in shards:
        steps = jnp.exp(jax.random.uniform(jax.random.fold_in(own, axis_at), (shards_of,), jnp.float32, least / len(shards), top_value / len(shards)))
        loudness = loudness * jnp.repeat(steps, extent[axis_at] // shards_of).reshape([-1 if axis == axis_at else 1 for axis in range(len(extent))])
    return loudness


def deal_out(stream_key, own, number, rows, count, top, reach, lean):
    order = jax.random.permutation(stream_key, count)
    heavy_load, ordinary = shares(count, rows * top, reach, lean, True), shares(count, rows * top, reach, lean, False)
    places = jnp.arange(count)

    def named(lengths, offset_by):
        used = int((lengths > 0).sum())
        fixed = max(1, used // 4)
        shifted = fixed + (places - fixed + offset_by * (used - fixed)) % max(1, count - fixed)
        return jnp.zeros((count,), jnp.int32).at[order[jnp.where(places < fixed, places, shifted)]].set(jnp.asarray(lengths, jnp.int32))

    lengths = jnp.where(number % 4 == 0, named(heavy_load, number // 4), named(ordinary, number - number // 4 - 1))
    mixed = jax.random.permutation(jax.random.fold_in(own, 3), count)
    source_of, taker = mixed[0:count // 2 * 2:2], mixed[1:count // 2 * 2:2]
    room = jnp.minimum(lengths[source_of] - 1, reach - lengths[taker]) // 2
    room = jnp.where((source_of == order[0]) | (taker == order[0]) | (lengths[taker] == 0), 0, jnp.maximum(room, 0))
    shifted = jax.random.randint(jax.random.fold_in(own, 4), (count // 2,), 0, 1 << 20) % (room + 1)
    lengths = lengths.at[source_of].add(-shifted).at[taker].add(shifted)
    labels = jnp.searchsorted(jnp.cumsum(lengths), jnp.arange(rows * top), side="right").astype(jnp.int32)
    table = labels.reshape(top, rows).T
    table = table[jax.random.permutation(jax.random.fold_in(own, 1), rows)]
    offset_by = jax.random.randint(jax.random.fold_in(own, 2), (rows, 1), 0, top)
    return jnp.take_along_axis(table, (jnp.arange(top)[None, :] + offset_by) % top, axis=1)


def shares(number_of, total, most, lean, full):
    weights = [(1 << 20) // math.isqrt(grade ** lean) + 1 for grade in range(1, number_of + 1)]
    largest = most if full else min(most, max(-(-total // number_of), total * weights[0] // sum(weights)))
    least = 1 if total - largest >= number_of - 1 else 0
    counts, spare = [largest] + [least] * (number_of - 1), total - largest - least * (number_of - 1)
    while spare > 0:
        candidates = [i for i in range(1, number_of) if counts[i] < largest] or [i for i in range(1, number_of) if counts[i] < most]
        whole, remaining = sum([weights[i] for i in candidates]), spare
        for i in candidates:
            more = min(most - counts[i], max(1, remaining * weights[i] // whole), spare)
            counts[i] = counts[i] + more
            spare = spare - more
    return np.array(counts)


def centred(stream_key, dims, spread, limit, split=(), kind=jnp.bfloat16):
    array = spread * jax.random.normal(stream_key, dims, jnp.float32)
    if split:
        array = array * block_scale(stream_key, dims, split, -0.22, 0.18)
    return jnp.clip(array, -limit, limit).astype(kind)


def setup_inputs(seed: int = 0) -> dict:
    key_list = jax.random.split(jax.random.key(seed), 9)
    theta = centred(key_list[0], (NBLK, BS, BS), 1.0, 6.0, ((0, 64),))
    left_env = centred(key_list[1], (TERMS, NSEC, BS, BS), BS ** -0.5, 0.5, ((0, 8), (1, 64)))
    right_env = centred(key_list[2], (TERMS, NSEC_R, BS, BS), BS ** -0.5, 0.5, ((0, 8), (1, 64)))
    coeff = centred(key_list[3], (TERMS, PHYS), 0.3, 1.8, ((0, 8),), jnp.float32)
    left_dims = draw_left_dims(jax.random.fold_in(key_list[8], 71), 0)
    right_dims = draw_right_dims(jax.random.fold_in(key_list[8], 71), 0)
    dest_dev_keys = jax.random.split(jax.random.fold_in(key_list[6], 1), NBLK // NB)
    dest_dev_turns = jax.random.permutation(jax.random.fold_in(key_list[6], 3), NBLK // NB)
    dest_dev = jax.vmap(lambda own, number: deal_out(jax.random.fold_in(key_list[6], 2), own, number, NB, N_TENSOR, 1, CAP, 2))(dest_dev_keys, dest_dev_turns).reshape((NBLK, 1))
    right_local = touch_ends(jax.random.randint(key_list[7], (NBLK,), 0, RSD), jax.random.fold_in(key_list[7], 1), 0, RSD - 1).astype(jnp.int32)
    return dict(theta=theta, left_env=left_env, right_env=right_env, coeff=coeff, left_dims=left_dims, right_dims=right_dims, dest_dev=dest_dev, right_local=right_local)


def reference(theta, left_env, right_env, coeff, left_dims, right_dims, dest_dev, right_local):
    block_ids = jnp.arange(NBLK, dtype=jnp.int32)
    left_sector = (block_ids // PHYS).astype(jnp.int32)
    phys_ids = (block_ids % PHYS).astype(jnp.int32)
    right_sector = (dest_dev[:, 0] * RSD + right_local).astype(jnp.int32)
    state_ids = jnp.arange(BS, dtype=jnp.int32)
    row_keep = (state_ids[None, :] < left_dims[left_sector][:, None]).astype(jnp.float32)
    col_keep = (state_ids[None, :] < right_dims[right_sector][:, None]).astype(jnp.float32)
    masked = theta.astype(jnp.float32) * row_keep[:, :, None] * col_keep[:, None, :]
    left_groups = left_env.reshape(N_TERM, TPG, NSEC, BS, BS)
    right_groups = right_env.reshape(N_TERM, TPG, NSEC_R, BS, BS)
    coeff_groups = coeff.reshape(N_TERM, TPG, PHYS)

    def group(total, pieces):
        left_part, right_part, coeff_part = pieces
        accum = jnp.zeros((NBLK, BS, BS), jnp.float32)
        for k in range(TPG):
            left_tiles = left_part[k][left_sector].astype(jnp.float32)
            product = jnp.einsum('nij,njk->nik', left_tiles, masked)
            carried = (coeff_part[k][phys_ids][:, None, None] * product).astype(jnp.bfloat16)
            right_tiles = right_part[k][right_sector].astype(jnp.float32)
            accum = accum + jnp.einsum('nij,nkj->nik', carried.astype(jnp.float32), right_tiles)
        partial_value = (accum * col_keep[:, None, :]).astype(jnp.bfloat16)
        return total + partial_value.astype(jnp.float32), None

    total, unused = lax.scan(group, jnp.zeros((NBLK, BS, BS), jnp.float32), (left_groups, right_groups, coeff_groups))
    return (total * row_keep[:, :, None]).astype(jnp.bfloat16)
```

```python
import jax
import jax.numpy as jnp
from jax import lax
from jax.experimental import pallas as pl
from jax.experimental.pallas import tpu as pltpu
from jax.sharding import Mesh, PartitionSpec as P

PHYS = 16
NT = (((1,), (1,)), ((), ()))
BF = jnp.bfloat16
F32 = jnp.float32


def shift(x, axis, by):
    count = lax.axis_size(axis)
    return lax.ppermute(x, axis, [(i, (i + by) % count) for i in range(count)])


def spread(x, axis, by):
    count = lax.axis_size(axis)
    pairs = []
    for i in range(count):
        pairs += [(2 * i, (i + by) % count * 2), (2 * i + 1, (i - by) % count * 2 + 1)]
    return lax.ppermute(x, (axis, "c"), pairs)


def both_ways(x, axis):
    up = down = x
    pieces, owners = [x], [0]
    for step in range(1, 4):
        up, down = shift(up, axis, 1), shift(down, axis, -1)
        pieces += [up, down]
        owners += [-step, step]
    return pieces + [shift(up, axis, 1)], owners + [-4]


def swap(x):
    return lax.ppermute(x, "c", [(0, 1), (1, 0)])


def contract_kernel(zi_ref, xc_ref, s_ref, c_ref, dims_ref, place_ref, th_own, th_sib, *rest):
    th_refs = (th_own, th_sib)
    l_refs, right = rest[:8], rest[8]
    out_ref, r_ref, th_ref, l_ref, a_ref, sems = rest[9:]
    copies = []

    def fetch(src, dst):
        copy = pltpu.make_async_copy(src, dst, sems.at[len(copies)])
        copy.start()
        copies.append(copy)

    for z in range(8):
        fetch(right.at[z], r_ref.at[z])
    for s in range(4):
        fetch(th_own.at[pl.ds(16 * s, 16)], th_ref.at[0, pl.ds(16 * s, 16)])
    for d, ref in enumerate(l_refs):
        for half in range(2):
            fetch(
                ref.at[half if d < 5 else 1 - half, pl.ds(0, 1024)], l_ref.at[half, place_ref[d]]
            )
    for s in range(4):
        fetch(th_sib.at[pl.ds(16 * s, 16)], th_ref.at[1, pl.ds(16 * s, 16)])
    for copy in copies[:8]:
        copy.wait()

    lane = lax.broadcasted_iota(jnp.int32, (128, 128), 1)
    for half in range(2):
        th, le = th_ref.at[half], l_ref.at[half]

        @pl.loop(0, 4)
        def sector(s):
            pltpu.make_async_copy(
                th_refs[half].at[pl.ds(16 * s, 16)],
                th_ref.at[half, pl.ds(16 * s, 16)],
                sems.at[(8, 28)[half] + s],
            ).wait()
            for pp in range(PHYS // 2):
                prods = []
                for e in range(2):
                    n = s * PHYS + 2 * pp + e
                    row = pl.multiple_of(s_ref[half, n] * 16, 16)
                    tile = r_ref[zi_ref[half, n], :, xc_ref[half, n], pl.ds(row, 16)]
                    prods.append(
                        lax.dot_general(
                            tile.reshape(128, 128), th[n], NT, preferred_element_type=F32
                        )
                    )
                for t in range(16):
                    pair = [
                        prods[e][t * 8 : t * 8 + 8] * c_ref[t, 2 * pp + e] for e in range(2)
                    ]
                    a_ref[pp * 16 : pp * 16 + 16, t * 128 : t * 128 + 128] = jnp.concatenate(
                        pair, axis=0
                    ).astype(BF)
            if half == 0:
                @pl.when(s == 0)
                def left_is_here():
                    for copy in copies[12:28]:
                        copy.wait()

            keep = lane < dims_ref[half, s]
            total = jnp.zeros((128, 128), F32)
            for y in range(8):
                tiles = [
                    jnp.where(
                        keep,
                        le[y, pl.ds(pl.multiple_of((t * 4 + s) * 128, 128), 128), :],
                        jnp.zeros((), BF),
                    )
                    for t in range(2)
                ]
                total += lax.dot_general(
                    a_ref[:, y * 256 : y * 256 + 256],
                    jnp.concatenate(tiles, axis=1),
                    NT,
                    preferred_element_type=F32,
                )
            out_ref[half, pl.ds(pl.multiple_of(s * 128, 128), 128), :] = jnp.where(
                keep, total, 0.0
            ).astype(BF)


def finish_kernel(place_ref, *refs):
    pieces, out_ref, rows_ref = refs[:8], refs[8], refs[9]
    eye = (
        lax.broadcasted_iota(jnp.int32, (128, 128), 0)
        == lax.broadcasted_iota(jnp.int32, (128, 128), 1)
    ).astype(F32).astype(BF)
    for d in range(8):
        row = pl.multiple_of(place_ref[d] * 16, 16)
        rows_ref[:, pl.ds(row, 16), :] = pieces[d][...]
    for n in range(out_ref.shape[0]):
        out_ref[n] = lax.dot_general(eye, rows_ref[n], NT, preferred_element_type=F32).astype(BF)


def on_device(theta, left_env, right_env, coeff, left_dims, right_dims, dest_dev, right_local):
    states = jnp.arange(128, dtype=jnp.int32)
    at_y, core = lax.axis_index("y"), lax.axis_index("c")
    first = core == 0
    toward = 2 * core - 1
    steps = [0] + [toward * k for k in (1, 2, 3, 4)] + [-toward * k for k in (1, 2, 3)]
    place = jnp.stack(
        [(at_y + d + 8) % 8 for d in steps]
    ).astype(jnp.int32)

    right_keep = states[None, :] < right_dims[:, None]
    right = jnp.where(
        right_keep[None, :, :, None] & right_keep[None, :, None, :], right_env, jnp.zeros((), BF)
    )
    right = right.reshape(2, 3, 8, 2, 8, 128).transpose(2, 3, 1, 0, 4, 5).reshape(8, 1, 2, 48, 128)
    block = dest_dev[:, 0] * 3 + right_local
    rows = []
    rest = coeff.reshape(1, 32)
    for _ in range(3):
        head = lax.reduce_precision(rest, 8, 7)
        rows.append(jnp.pad(head, ((0, 0), (0, 96))))
        rest = rest - head
    rows.append(jnp.pad(block.astype(F32)[None, :], ((0, 0), (0, 64))))
    rows.append(jnp.pad(left_dims.astype(F32)[None, :], ((0, 11), (0, 124))))
    extra = jnp.concatenate(rows, axis=0).astype(BF)
    left = jnp.concatenate([left_env.reshape(1024, 128), extra], axis=0)
    right = jnp.broadcast_to(right, (8, 4, 2, 48, 128)).reshape(64, 48, 128)
    right = lax.all_to_all(right, ("y", "x", "c"), split_axis=0, concat_axis=0, tiled=True)
    left, right = lax.optimization_barrier((left, right))
    right = lax.all_gather(right.reshape(8, 8, 48, 128), "z")
    pair = jnp.stack([left, swap(left)])
    theta_sib = swap(theta)
    lefts = [pair] + [spread(pair, "y", k) for k in range(1, 5)]
    lefts += [swap(piece) for piece in lefts[1:4]]

    weights = jnp.stack(
        [piece[int(d > 4), 1024:1027, :32].astype(F32) for d, piece in enumerate(lefts)]
    )
    weights = (weights[:, 0] + weights[:, 1] + weights[:, 2]).reshape(8, 1, 2, PHYS)
    here = place[:, None] == jnp.arange(8, dtype=jnp.int32)[None, :]
    weights = jnp.sum(jnp.where(here[:, :, None, None], weights, 0.0), axis=0).reshape(16, PHYS)
    blocks = jnp.stack([block, lefts[0][1, 1027, :64].astype(F32).astype(jnp.int32)])
    dims = jnp.stack([left_dims, lefts[0][1, 1028, :4].astype(F32).astype(jnp.int32)])

    vmem = pl.BlockSpec(memory_space=pltpu.VMEM)
    smem = pl.BlockSpec(memory_space=pltpu.SMEM)
    hbm = pl.BlockSpec(memory_space=pl.ANY)
    part = pl.pallas_call(
        contract_kernel,
        out_shape=jax.ShapeDtypeStruct((2, 512, 128), BF),
        in_specs=[smem] * 6 + [hbm] * 11,
        out_specs=vmem,
        scratch_shapes=[
            pltpu.VMEM((8, 8, 8, 48, 128), BF),
            pltpu.VMEM((2, 64, 128, 128), BF),
            pltpu.VMEM((2, 8, 1024, 128), BF),
            pltpu.VMEM((128, 2048), BF),
            pltpu.SemaphoreType.DMA((32,)),
        ],
        compiler_params=pltpu.CompilerParams(vmem_limit_bytes=56 * 2**20),
        cost_estimate=pl.CostEstimate(flops=1 << 30, bytes_accessed=16 << 20, transcendentals=0),
    )(
        blocks // 24,
        blocks // 3 % 8,
        blocks % 3,
        weights,
        dims,
        place,
        theta,
        theta_sib,
        *lefts,
        right,
    )

    mine = part[0].reshape(64, 8, 128)
    other = swap(part[1]).reshape(64, 8, 128)
    piece = jnp.concatenate(
        [jnp.where(first, mine, other), jnp.where(first, other, mine)], axis=1
    )
    pieces, owners = both_ways(piece, "y")
    place = jnp.stack([(at_y + o + 8) % 8 for o in owners]).astype(jnp.int32)
    return pl.pallas_call(
        finish_kernel,
        grid=(4,),
        out_shape=jax.ShapeDtypeStruct((64, 128, 128), BF),
        in_specs=[smem] + [pl.BlockSpec((16, 16, 128), lambda i: (i, 0, 0))] * 8,
        out_specs=pl.BlockSpec((16, 128, 128), lambda i: (i, 0, 0)),
        scratch_shapes=[pltpu.VMEM((16, 128, 128), BF)],
        compiler_params=pltpu.CompilerParams(vmem_limit_bytes=16 * 2**20),
        cost_estimate=pl.CostEstimate(flops=1 << 28, bytes_accessed=4 << 20, transcendentals=0),
    )(place, *pieces)


def solution(mesh):
    grid = Mesh(mesh.devices.reshape(8, 8, 4, 2), ("y", "z", "x", "c"))
    tensor = ("z", "x", "c")
    in_specs = (
        P(tensor, None, None),
        P("y", tensor, None, None),
        P("y", tensor, None, None),
        P("y", None),
        P(tensor),
        P(tensor),
        P(tensor, None),
        P(tensor),
    )
    return jax.shard_map(
        on_device, mesh=grid, in_specs=in_specs, out_specs=P(tensor, None, None), check_vma=False
    )
```

```python
import jax
import jax.numpy as jnp
from jax import lax
from jax.experimental import pallas as pl
from jax.experimental.pallas import tpu as pltpu
from jax.sharding import Mesh, PartitionSpec as P

PHYS = 16
NT = (((1,), (1,)), ((), ()))
BF = jnp.bfloat16
F32 = jnp.float32


def shift(x, axis, by):
    count = lax.axis_size(axis)
    return lax.ppermute(x, axis, [(i, (i + by) % count) for i in range(count)])


def both_ways(x, axis):
    up = down = x
    pieces, owners = [x], [0]
    for step in range(1, 4):
        up, down = shift(up, axis, 1), shift(down, axis, -1)
        pieces += [up, down]
        owners += [-step, step]
    return pieces + [shift(up, axis, 1)], owners + [-4]


def swap(x):
    return lax.ppermute(x, "c", [(0, 1), (1, 0)])


def flip(rows):
    eye = (
        lax.broadcasted_iota(jnp.int32, (128, 128), 0)
        == lax.broadcasted_iota(jnp.int32, (128, 128), 1)
    ).astype(F32).astype(BF)
    return lax.dot_general(eye, rows, NT, preferred_element_type=F32).astype(BF)


def theta_kernel(th_own, th_sib, out_ref):
    for half, th in enumerate((th_own, th_sib)):
        @pl.loop(0, 8)
        def some(i):
            for k in range(8):
                out_ref[half, i * 8 + k] = flip(th[i * 8 + k])


def left_kernel(l_own, l_sib, out_ref, sems):
    copies = [
        pltpu.make_async_copy(ref.at[y], out_ref.at[half, y], sems.at[half, y])
        for half, ref in enumerate((l_own, l_sib))
        for y in range(8)
    ]
    for copy in copies:
        copy.start()
    for copy in copies:
        copy.wait()


def contract_kernel(zi_ref, xc_ref, s_ref, c_ref, dims_ref, place_ref, th_ref, l_ref, *rest):
    two, one = rest[0], rest[1:6]
    out_refs, (r_ref, a_ref, sems) = rest[6:8], rest[8:]
    copies = []

    def fetch(src, dst):
        copy = pltpu.make_async_copy(src, dst, sems.at[len(copies)])
        copy.start()
        copies.append(copy)

    for z in range(8):
        fetch(two.at[z], r_ref.at[z, :, :, :, pl.ds(0, 32)])
    for d in range(3):
        fetch(one[d], r_ref.at[:, place_ref[d], :, :, pl.ds(32, 16)])
    for d in range(2):
        fetch(one[3 + d], r_ref.at[pl.ds(4 * d, 4), place_ref[3], :, :, pl.ds(32, 16)])
    for copy in copies:
        copy.wait()

    lane = lax.broadcasted_iota(jnp.int32, (128, 128), 1)
    for half in range(2):
        @pl.loop(0, 4, unroll=4)
        def sector(s):
            for pp in range(PHYS // 2):
                prods = []
                for e in range(2):
                    n = s * PHYS + 2 * pp + e
                    row = pl.multiple_of(s_ref[half, n] * 16, 16)
                    xc = xc_ref[half, n]
                    tile = r_ref[zi_ref[half, n], xc // 2, :, xc % 2, pl.ds(row, 16)]
                    prods.append(
                        jnp.dot(
                            tile.reshape(128, 128), th_ref[half, n], preferred_element_type=F32
                        )
                    )
                for t in range(16):
                    pair = [
                        prods[e][t * 8 : t * 8 + 8] * c_ref[t, 2 * pp + e] for e in range(2)
                    ]
                    a_ref[s, pp * 16 : pp * 16 + 16, t * 128 : t * 128 + 128] = jnp.concatenate(
                        pair, axis=0
                    ).astype(BF)
            keep = lane < dims_ref[half, s]
            total = jnp.zeros((128, 128), F32)
            for y in range(8):
                tiles = [
                    jnp.where(keep, l_ref[half, y, t, s], jnp.zeros((), BF)) for t in range(2)
                ]
                total += lax.dot_general(
                    a_ref[s, :, y * 256 : y * 256 + 256],
                    jnp.concatenate(tiles, axis=1),
                    NT,
                    preferred_element_type=F32,
                )
            out_refs[half][pl.ds(pl.multiple_of(s * 128, 128), 128), :] = jnp.where(
                keep, total, 0.0
            ).astype(BF)


def finish_kernel(place_ref, *refs):
    pieces, out_ref, rows_ref = refs[:8], refs[8], refs[9]
    for d in range(8):
        row = pl.multiple_of(place_ref[d] * 16, 16)
        rows_ref[:, pl.ds(row, 16), :] = pieces[d][...]
    for n in range(out_ref.shape[0]):
        out_ref[n] = flip(rows_ref[n])


def on_device(theta, left_env, right_env, coeff, left_dims, right_dims, dest_dev, right_local):
    states = jnp.arange(128, dtype=jnp.int32)
    at_y, at_x = lax.axis_index("y"), lax.axis_index("x")
    first = lax.axis_index("c") == 0

    right_keep = states[None, :] < right_dims[:, None]
    right = jnp.where(
        right_keep[None, :, :, None] & right_keep[None, :, None, :], right_env, jnp.zeros((), BF)
    )
    right = right.reshape(2, 3, 8, 2, 8, 128).transpose(2, 3, 1, 0, 4, 5).reshape(8, 1, 2, 48, 128)
    block = dest_dev[:, 0] * 3 + right_local
    facts = jnp.stack([block, jnp.pad(left_dims, (0, 60))])
    facts = jnp.stack([facts, swap(facts)])
    blocks, dims = facts[:, 0], facts[:, 1, :4]
    parts = []
    rest = coeff.reshape(1, 32)
    for _ in range(3):
        head = lax.reduce_precision(rest, 8, 7)
        parts.append(head.astype(BF))
        rest = rest - head
    extra = jnp.pad(jnp.concatenate(parts, axis=0), ((0, 13), (0, 96)))
    right = jnp.concatenate(
        [right.reshape(16, 48, 128), jnp.broadcast_to(extra[None], (16, 16, 128))], axis=1
    )
    left_own = lax.all_gather(left_env, "y")
    right = lax.all_to_all(
        right, ("y", "c"), split_axis=0, concat_axis=0, tiled=True
    ).reshape(8, 2, 64, 128)
    two = jnp.broadcast_to(right[None, :, :, :32], (4, 8, 2, 32, 128))
    two = lax.all_to_all(two, "x", split_axis=0, concat_axis=0, tiled=True)
    one, two = lax.optimization_barrier((right[:, :, 32:48], two))
    two = lax.all_gather(two, "z")
    one = jnp.broadcast_to(one[None], (8, 8, 2, 16, 128))
    one = lax.all_to_all(one, "z", split_axis=0, concat_axis=0, tiled=True)
    theta_sib = swap(theta)
    weights = right[:, 0, 48:51, :32].astype(F32)
    weights = (weights[:, 0] + weights[:, 1] + weights[:, 2]).reshape(16, PHYS)
    vmem = pl.BlockSpec(memory_space=pltpu.VMEM)
    smem = pl.BlockSpec(memory_space=pltpu.SMEM)
    hbm = pl.BlockSpec(memory_space=pl.ANY)

    def settings(mib, flops, traffic):
        return dict(
            compiler_params=pltpu.CompilerParams(vmem_limit_bytes=mib * 2**20),
            cost_estimate=pl.CostEstimate(
                flops=flops, bytes_accessed=traffic << 20, transcendentals=0
            ),
        )

    flipped = pl.pallas_call(
        theta_kernel,
        out_shape=jax.ShapeDtypeStruct((2, 64, 128, 128), BF),
        in_specs=[vmem] * 2,
        out_specs=vmem,
        **settings(32, 1 << 29, 8),
    )(theta, theta_sib)
    one, flipped, blocks, dims, weights = lax.optimization_barrier(
        (one, flipped, blocks, dims, weights)
    )
    ones = [
        one,
        shift(one, "x", 1),
        shift(one, "x", -1),
        shift(one[:4], "x", 2),
        shift(one[4:], "x", -2),
    ]
    place = jnp.stack([(at_x + d) % 4 for d in (0, 3, 1, 2)]).astype(jnp.int32)

    left_own, _ = lax.optimization_barrier((left_own, ones[1:]))
    left_sib = swap(left_own)
    lefts = pl.pallas_call(
        left_kernel,
        out_shape=jax.ShapeDtypeStruct((2, *left_own.shape), BF),
        in_specs=[hbm] * 2,
        out_specs=vmem,
        scratch_shapes=[pltpu.SemaphoreType.DMA((2, 8))],
        **settings(32, 0, 8),
    )(left_own, left_sib)
    mine, other = pl.pallas_call(
        contract_kernel,
        out_shape=(jax.ShapeDtypeStruct((512, 128), BF),) * 2,
        in_specs=[smem] * 6 + [vmem] * 2 + [hbm] * 6,
        out_specs=(vmem, vmem),
        scratch_shapes=[
            pltpu.VMEM((8, 4, 8, 2, 48, 128), BF),
            pltpu.VMEM((4, 128, 2048), BF),
            pltpu.SemaphoreType.DMA((13,)),
        ],
        **settings(52, 1 << 30, 8),
    )(blocks // 24, blocks // 3 % 8, blocks % 3, weights, dims, place, flipped, lefts, two, *ones)

    mine = mine.reshape(64, 8, 128)
    other = swap(other).reshape(64, 8, 128)
    piece = jnp.concatenate(
        [jnp.where(first, mine, other), jnp.where(first, other, mine)], axis=1
    )
    pieces, owners = both_ways(piece, "y")
    place = jnp.stack([(at_y + o + 8) % 8 for o in owners]).astype(jnp.int32)
    return pl.pallas_call(
        finish_kernel,
        grid=(4,),
        out_shape=jax.ShapeDtypeStruct((64, 128, 128), BF),
        in_specs=[smem] + [pl.BlockSpec((16, 16, 128), lambda i: (i, 0, 0))] * 8,
        out_specs=pl.BlockSpec((16, 128, 128), lambda i: (i, 0, 0)),
        scratch_shapes=[pltpu.VMEM((16, 128, 128), BF)],
        compiler_params=pltpu.CompilerParams(vmem_limit_bytes=16 * 2**20),
        cost_estimate=pl.CostEstimate(flops=1 << 28, bytes_accessed=4 << 20, transcendentals=0),
    )(place, *pieces)


def solution(mesh):
    grid = Mesh(mesh.devices.reshape(8, 8, 4, 2), ("y", "z", "x", "c"))
    tensor = ("z", "x", "c")
    in_specs = (
        P(tensor, None, None),
        P("y", tensor, None, None),
        P("y", tensor, None, None),
        P("y", None),
        P(tensor),
        P(tensor),
        P(tensor, None),
        P(tensor),
    )
    return jax.shard_map(
        on_device, mesh=grid, in_specs=in_specs, out_specs=P(tensor, None, None), check_vma=False
    )
```

```python
import jax
import jax.numpy as jnp
from jax import lax
from jax.experimental import pallas as pl
from jax.experimental.pallas import tpu as pltpu
from jax.sharding import Mesh, PartitionSpec as P

PHYS = 16
SPLIT = 7
NT = (((1,), (1,)), ((), ()))
BF = jnp.bfloat16
F32 = jnp.float32


def shift(x, axis, by):
    count = lax.axis_size(axis)
    return lax.ppermute(x, axis, [(i, (i + by) % count) for i in range(count)])


def both_ways(x, axis):
    up = down = x
    pieces, owners = [x], [0]
    for step in range(1, 4):
        up, down = shift(up, axis, 1), shift(down, axis, -1)
        pieces += [up, down]
        owners += [-step, step]
    return pieces + [shift(up, axis, 1)], owners + [-4]


def swap(x):
    return lax.ppermute(x, "c", [(0, 1), (1, 0)])


def flip(rows):
    eye = (
        lax.broadcasted_iota(jnp.int32, (128, 128), 0)
        == lax.broadcasted_iota(jnp.int32, (128, 128), 1)
    ).astype(F32).astype(BF)
    return lax.dot_general(eye, rows, NT, preferred_element_type=F32).astype(BF)


def theta_kernel(th_own, th_sib, out_ref):
    for half, th in enumerate((th_own, th_sib)):
        @pl.loop(0, 8)
        def some(i):
            for k in range(8):
                out_ref[half, i * 8 + k] = flip(th[i * 8 + k])


def contract_kernel(zi_ref, xc_ref, s_ref, c_ref, dims_ref, place_ref, *rest):
    theta, lefts, two, one = rest[0], rest[1:3], rest[3], rest[4:9]
    out_refs, (r_ref, th_ref, l_ref, a_ref, sems) = rest[9:11], rest[11:]
    copies = []

    def fetch(src, dst):
        copy = pltpu.make_async_copy(src, dst, sems.at[len(copies)])
        copy.start()
        copies.append(copy)

    for z in range(8):
        fetch(two.at[z, :, pl.ds(0, 8)], r_ref.at[z, :, 0])
        fetch(two.at[z, :, pl.ds(8, SPLIT)], r_ref.at[z, :, 1, pl.ds(0, SPLIT)])
    for d in range(5):
        z = pl.ds(4 * (d - 3), 4) if d > 2 else pl.ds(0, 8)
        x = place_ref[min(d, 3)]
        fetch(one[d].at[:, pl.ds(0, 8)], r_ref.at[z, x, 2])
        fetch(one[d].at[:, pl.ds(8, 8 - SPLIT)], r_ref.at[z, x, 1, pl.ds(SPLIT, 8 - SPLIT)])
    for half in range(2):
        fetch(theta.at[half], th_ref.at[half])
        fetch(lefts[half], l_ref.at[half])

    lane = lax.broadcasted_iota(jnp.int32, (128, 128), 1)
    for half in range(2):
        for copy in copies[28 * half : 28 + 2 * half]:
            copy.wait()

        @pl.loop(0, 4, unroll=4)
        def sector(s):
            for pp in range(PHYS // 2):
                prods = []
                for e in range(2):
                    n = s * PHYS + 2 * pp + e
                    xc = xc_ref[half, n]
                    tile = r_ref[zi_ref[half, n], xc // 2, s_ref[half, n], :, xc % 2]
                    prods.append(
                        jnp.dot(
                            tile.reshape(128, 128), th_ref[half, n], preferred_element_type=F32
                        )
                    )
                for t in range(16):
                    pair = [
                        prods[e][t * 8 : t * 8 + 8] * c_ref[t, 2 * pp + e] for e in range(2)
                    ]
                    a_ref[s, pp * 16 : pp * 16 + 16, t * 128 : t * 128 + 128] = jnp.concatenate(
                        pair, axis=0
                    ).astype(BF)
            keep = lane < dims_ref[half, s]
            total = jnp.zeros((128, 128), F32)
            for y in range(8):
                tiles = [
                    jnp.where(keep, l_ref[half, y, t, s], jnp.zeros((), BF)) for t in range(2)
                ]
                total += lax.dot_general(
                    a_ref[s, :, y * 256 : y * 256 + 256],
                    jnp.concatenate(tiles, axis=1),
                    NT,
                    preferred_element_type=F32,
                )
            out_refs[half][pl.ds(pl.multiple_of(s * 128, 128), 128), :] = jnp.where(
                keep, total, 0.0
            ).astype(BF)


def finish_kernel(place_ref, *refs):
    pieces, out_ref, rows_ref = refs[:8], refs[8], refs[9]
    for d in range(8):
        row = pl.multiple_of(place_ref[d] * 16, 16)
        rows_ref[:, pl.ds(row, 16), :] = pieces[d][...]
    for n in range(out_ref.shape[0]):
        out_ref[n] = flip(rows_ref[n])


def on_device(theta, left_env, right_env, coeff, left_dims, right_dims, dest_dev, right_local):
    states = jnp.arange(128, dtype=jnp.int32)
    at_y, at_x = lax.axis_index("y"), lax.axis_index("x")
    first = lax.axis_index("c") == 0

    right_keep = states[None, :] < right_dims[:, None]
    right = jnp.where(
        right_keep[None, :, :, None] & right_keep[None, :, None, :], right_env, jnp.zeros((), BF)
    )
    right = right.reshape(2, 3, 8, 2, 8, 128).transpose(2, 3, 1, 0, 4, 5).reshape(8, 1, 2, 48, 128)
    block = dest_dev[:, 0] * 3 + right_local
    facts = jnp.stack([block, jnp.pad(left_dims, (0, 60))])
    facts = jnp.stack([facts, swap(facts)])
    blocks, dims = facts[:, 0], facts[:, 1, :4]
    parts = []
    rest = coeff.reshape(1, 32)
    for _ in range(3):
        head = lax.reduce_precision(rest, 8, 7)
        parts.append(head.astype(BF))
        rest = rest - head
    extra = jnp.pad(jnp.concatenate(parts, axis=0), ((0, 13), (0, 96)))
    right = jnp.concatenate(
        [right.reshape(16, 48, 128), jnp.broadcast_to(extra[None], (16, 16, 128))], axis=1
    )
    left_own = lax.all_gather(left_env, "y")
    right = lax.all_to_all(
        right, ("y", "c"), split_axis=0, concat_axis=0, tiled=True
    ).reshape(8, 2, 64, 128)
    two = jnp.concatenate([right[:, :, :16], right[:SPLIT, :, 16:32]], axis=0)
    one = jnp.concatenate([right[:, :, 32:48], right[SPLIT:, :, 16:32]], axis=0)
    two = jnp.broadcast_to(two[None], (4, *two.shape))
    two = lax.all_to_all(two, "x", split_axis=0, concat_axis=0, tiled=True)
    one, two = lax.optimization_barrier((one, two))
    two = lax.all_gather(two, "z")
    one = jnp.broadcast_to(one[None], (8, *one.shape))
    one = lax.all_to_all(one, "z", split_axis=0, concat_axis=0, tiled=True)
    theta_sib = swap(theta)
    weights = right[:, 0, 48:51, :32].astype(F32)
    weights = (weights[:, 0] + weights[:, 1] + weights[:, 2]).reshape(16, PHYS)
    vmem = pl.BlockSpec(memory_space=pltpu.VMEM)
    smem = pl.BlockSpec(memory_space=pltpu.SMEM)
    hbm = pl.BlockSpec(memory_space=pl.ANY)

    def settings(mib, flops, traffic):
        return dict(
            compiler_params=pltpu.CompilerParams(vmem_limit_bytes=mib * 2**20),
            cost_estimate=pl.CostEstimate(
                flops=flops, bytes_accessed=traffic << 20, transcendentals=0
            ),
        )

    flipped = pl.pallas_call(
        theta_kernel,
        out_shape=jax.ShapeDtypeStruct((2, 64, 128, 128), BF),
        in_specs=[vmem] * 2,
        out_specs=vmem,
        **settings(32, 1 << 29, 8),
    )(theta, theta_sib)
    one, flipped, blocks, dims, weights = lax.optimization_barrier(
        (one, flipped, blocks, dims, weights)
    )
    ones = [
        one,
        shift(one, "x", 1),
        shift(one, "x", -1),
        shift(one[:4], "x", 2),
        shift(one[4:], "x", -2),
    ]
    place = jnp.stack([(at_x + d) % 4 for d in (0, 3, 1, 2)]).astype(jnp.int32)

    left_own, _ = lax.optimization_barrier((left_own, one))
    left_sib = swap(left_own)
    mine, other = pl.pallas_call(
        contract_kernel,
        out_shape=(jax.ShapeDtypeStruct((512, 128), BF),) * 2,
        in_specs=[smem] * 6 + [hbm] * 9,
        out_specs=(vmem, vmem),
        scratch_shapes=[
            pltpu.VMEM((8, 4, 3, 8, 2, 16, 128), BF),
            pltpu.VMEM((2, 64, 128, 128), BF),
            pltpu.VMEM((2, 8, 2, 4, 128, 128), BF),
            pltpu.VMEM((4, 128, 2048), BF),
            pltpu.SemaphoreType.DMA((30,)),
        ],
        **settings(56, 1 << 30, 8),
    )(blocks // 24, blocks // 3 % 8, blocks % 3, weights, dims, place, flipped, left_own, left_sib, two, *ones)

    mine = mine.reshape(64, 8, 128)
    other = swap(other).reshape(64, 8, 128)
    piece = jnp.concatenate(
        [jnp.where(first, mine, other), jnp.where(first, other, mine)], axis=1
    )
    pieces, owners = both_ways(piece, "y")
    place = jnp.stack([(at_y + o + 8) % 8 for o in owners]).astype(jnp.int32)
    return pl.pallas_call(
        finish_kernel,
        grid=(2,),
        out_shape=jax.ShapeDtypeStruct((64, 128, 128), BF),
        in_specs=[smem] + [pl.BlockSpec((32, 16, 128), lambda i: (i, 0, 0))] * 8,
        out_specs=pl.BlockSpec((32, 128, 128), lambda i: (i, 0, 0)),
        scratch_shapes=[pltpu.VMEM((32, 128, 128), BF)],
        compiler_params=pltpu.CompilerParams(vmem_limit_bytes=16 * 2**20),
        cost_estimate=pl.CostEstimate(flops=1 << 28, bytes_accessed=4 << 20, transcendentals=0),
    )(place, *pieces)


def solution(mesh):
    grid = Mesh(mesh.devices.reshape(8, 8, 4, 2), ("y", "z", "x", "c"))
    tensor = ("z", "x", "c")
    in_specs = (
        P(tensor, None, None),
        P("y", tensor, None, None),
        P("y", tensor, None, None),
        P("y", None),
        P(tensor),
        P(tensor),
        P(tensor, None),
        P(tensor),
    )
    return jax.shard_map(
        on_device, mesh=grid, in_specs=in_specs, out_specs=P(tensor, None, None), check_vma=False
    )
```

```python
import jax
import jax.numpy as jnp
from jax import lax
from jax.experimental import pallas as pl
from jax.experimental.pallas import tpu as pltpu
from jax.sharding import Mesh, PartitionSpec as P

PHYS = 16
SPLIT = 7
NT = (((1,), (1,)), ((), ()))
BF = jnp.bfloat16
F32 = jnp.float32


def shift(x, axis, by):
    count = lax.axis_size(axis)
    return lax.ppermute(x, axis, [(i, (i + by) % count) for i in range(count)])


def both_ways(x, axis):
    up, down = shift(x, axis, 1), shift(x, axis, -1)
    up2, up3 = shift(up, axis, 1), shift(up, axis, 2)
    down2, down3 = shift(down, axis, -1), shift(down, axis, -2)
    far = shift(up3, axis, 1)
    pieces = lax.optimization_barrier([up, down, up2, down2, up3, down3, far])
    return [x, *pieces], [0, -1, 1, -2, 2, -3, 3, -4]


def swap(x):
    return lax.ppermute(x, "c", [(0, 1), (1, 0)])


def flip(rows):
    eye = (
        lax.broadcasted_iota(jnp.int32, (128, 128), 0)
        == lax.broadcasted_iota(jnp.int32, (128, 128), 1)
    ).astype(F32).astype(BF)
    return lax.dot_general(eye, rows, NT, preferred_element_type=F32).astype(BF)


def theta_kernel(th_own, th_sib, out_ref):
    for half, th in enumerate((th_own, th_sib)):
        @pl.loop(0, 8)
        def some(i):
            for k in range(8):
                out_ref[half, i * 8 + k] = flip(th[i * 8 + k])


def contract_kernel(zi_ref, xc_ref, s_ref, c_ref, dims_ref, place_ref, *rest):
    theta, lefts, two, one = rest[0], rest[1:3], rest[3], rest[4:9]
    out_refs, (r_ref, th_ref, l_ref, a_ref, sems) = rest[9:11], rest[11:]
    copies = []

    def fetch(src, dst):
        copy = pltpu.make_async_copy(src, dst, sems.at[len(copies)])
        copy.start()
        copies.append(copy)

    for z in range(8):
        fetch(two.at[z, :, pl.ds(0, 8)], r_ref.at[z, :, 0])
        fetch(two.at[z, :, pl.ds(8, SPLIT)], r_ref.at[z, :, 1, pl.ds(0, SPLIT)])
    for d in range(5):
        z = pl.ds(4 * (d - 3), 4) if d > 2 else pl.ds(0, 8)
        x = place_ref[min(d, 3)]
        fetch(one[d].at[:, pl.ds(0, 8)], r_ref.at[z, x, 2])
        fetch(one[d].at[:, pl.ds(8, 8 - SPLIT)], r_ref.at[z, x, 1, pl.ds(SPLIT, 8 - SPLIT)])
    for half in range(2):
        fetch(theta.at[half], th_ref.at[half])
        fetch(lefts[half], l_ref.at[half])

    lane = lax.broadcasted_iota(jnp.int32, (128, 128), 1)
    for half in range(2):
        for copy in copies[28 * half : 28 + 2 * half]:
            copy.wait()

        @pl.loop(0, 4, unroll=4)
        def sector(s):
            for pp in range(PHYS // 2):
                prods = []
                for e in range(2):
                    n = s * PHYS + 2 * pp + e
                    xc = xc_ref[half, n]
                    tile = r_ref[zi_ref[half, n], xc // 2, s_ref[half, n], :, xc % 2]
                    prods.append(
                        jnp.dot(
                            tile.reshape(128, 128), th_ref[half, n], preferred_element_type=F32
                        )
                    )
                for t in range(16):
                    pair = [
                        prods[e][t * 8 : t * 8 + 8] * c_ref[t, 2 * pp + e] for e in range(2)
                    ]
                    a_ref[s, pp * 16 : pp * 16 + 16, t * 128 : t * 128 + 128] = jnp.concatenate(
                        pair, axis=0
                    ).astype(BF)
            keep = lane < dims_ref[half, s]
            total = jnp.zeros((128, 128), F32)
            for y in range(8):
                tiles = [
                    jnp.where(keep, l_ref[half, y, t, s], jnp.zeros((), BF)) for t in range(2)
                ]
                total += lax.dot_general(
                    a_ref[s, :, y * 256 : y * 256 + 256],
                    jnp.concatenate(tiles, axis=1),
                    NT,
                    preferred_element_type=F32,
                )
            out_refs[half][pl.ds(pl.multiple_of(s * 128, 128), 128), :] = jnp.where(
                keep, total, 0.0
            ).astype(BF)


def finish_kernel(place_ref, *refs):
    pieces, out_ref, rows_ref = refs[:8], refs[8], refs[9]
    for d in range(8):
        row = pl.multiple_of(place_ref[d] * 16, 16)
        rows_ref[:, pl.ds(row, 16), :] = pieces[d][...]
    for n in range(out_ref.shape[0]):
        out_ref[n] = flip(rows_ref[n])


def on_device(theta, left_env, right_env, coeff, left_dims, right_dims, dest_dev, right_local):
    states = jnp.arange(128, dtype=jnp.int32)
    at_y, at_x = lax.axis_index("y"), lax.axis_index("x")
    first = lax.axis_index("c") == 0

    right_keep = states[None, :] < right_dims[:, None]
    right = jnp.where(
        right_keep[None, :, :, None] & right_keep[None, :, None, :], right_env, jnp.zeros((), BF)
    )
    right = right.reshape(2, 3, 8, 2, 8, 128).transpose(2, 3, 1, 0, 4, 5).reshape(8, 1, 2, 48, 128)
    block = dest_dev[:, 0] * 3 + right_local
    facts = jnp.stack([block, jnp.pad(left_dims, (0, 60))])
    facts = jnp.stack([facts, swap(facts)])
    blocks, dims = facts[:, 0], facts[:, 1, :4]
    parts = []
    rest = coeff.reshape(1, 32)
    for _ in range(3):
        head = lax.reduce_precision(rest, 8, 7)
        parts.append(head.astype(BF))
        rest = rest - head
    extra = jnp.pad(jnp.concatenate(parts, axis=0), ((0, 13), (0, 96)))
    right = jnp.concatenate(
        [right.reshape(16, 48, 128), jnp.broadcast_to(extra[None], (16, 16, 128))], axis=1
    )
    left_own = lax.all_gather(left_env, "y")
    right = lax.all_to_all(
        right, ("y", "c"), split_axis=0, concat_axis=0, tiled=True
    ).reshape(8, 2, 64, 128)
    two = jnp.concatenate([right[:, :, :16], right[:SPLIT, :, 16:32]], axis=0)
    one = jnp.concatenate([right[:, :, 32:48], right[SPLIT:, :, 16:32]], axis=0)
    two = jnp.broadcast_to(two[None], (4, *two.shape))
    two = lax.all_to_all(two, "x", split_axis=0, concat_axis=0, tiled=True)
    one, two = lax.optimization_barrier((one, two))
    two = lax.all_gather(two, "z")
    one = jnp.broadcast_to(one[None], (8, *one.shape))
    one = lax.all_to_all(one, "z", split_axis=0, concat_axis=0, tiled=True)
    theta_sib = swap(theta)
    weights = right[:, 0, 48:51, :32].astype(F32)
    weights = (weights[:, 0] + weights[:, 1] + weights[:, 2]).reshape(16, PHYS)
    vmem = pl.BlockSpec(memory_space=pltpu.VMEM)
    smem = pl.BlockSpec(memory_space=pltpu.SMEM)
    hbm = pl.BlockSpec(memory_space=pl.ANY)

    def settings(mib, flops, traffic):
        return dict(
            compiler_params=pltpu.CompilerParams(vmem_limit_bytes=mib * 2**20),
            cost_estimate=pl.CostEstimate(
                flops=flops, bytes_accessed=traffic << 20, transcendentals=0
            ),
        )

    flipped = pl.pallas_call(
        theta_kernel,
        out_shape=jax.ShapeDtypeStruct((2, 64, 128, 128), BF),
        in_specs=[vmem] * 2,
        out_specs=vmem,
        **settings(32, 1 << 29, 8),
    )(theta, theta_sib)
    one, flipped, blocks, dims, weights = lax.optimization_barrier(
        (one, flipped, blocks, dims, weights)
    )
    ones = [
        one,
        shift(one, "x", 1),
        shift(one, "x", -1),
        shift(one[:4], "x", 2),
        shift(one[4:], "x", -2),
    ]
    place = jnp.stack([(at_x + d) % 4 for d in (0, 3, 1, 2)]).astype(jnp.int32)

    left_own, _ = lax.optimization_barrier((left_own, one))
    left_sib = swap(left_own)
    mine, other = pl.pallas_call(
        contract_kernel,
        out_shape=(jax.ShapeDtypeStruct((512, 128), BF),) * 2,
        in_specs=[smem] * 6 + [hbm] * 9,
        out_specs=(vmem, vmem),
        scratch_shapes=[
            pltpu.VMEM((8, 4, 3, 8, 2, 16, 128), BF),
            pltpu.VMEM((2, 64, 128, 128), BF),
            pltpu.VMEM((2, 8, 2, 4, 128, 128), BF),
            pltpu.VMEM((4, 128, 2048), BF),
            pltpu.SemaphoreType.DMA((30,)),
        ],
        **settings(56, 1 << 30, 8),
    )(blocks // 24, blocks // 3 % 8, blocks % 3, weights, dims, place, flipped, left_own, left_sib, two, *ones)

    mine = mine.reshape(64, 8, 128)
    other = swap(other).reshape(64, 8, 128)
    piece = jnp.concatenate(
        [jnp.where(first, mine, other), jnp.where(first, other, mine)], axis=1
    )
    piece = lax.optimization_barrier(piece)
    pieces, owners = both_ways(piece, "y")
    place = jnp.stack([(at_y + o + 8) % 8 for o in owners]).astype(jnp.int32)
    return pl.pallas_call(
        finish_kernel,
        grid=(2,),
        out_shape=jax.ShapeDtypeStruct((64, 128, 128), BF),
        in_specs=[smem] + [pl.BlockSpec((32, 16, 128), lambda i: (i, 0, 0))] * 8,
        out_specs=pl.BlockSpec((32, 128, 128), lambda i: (i, 0, 0)),
        scratch_shapes=[pltpu.VMEM((32, 128, 128), BF)],
        compiler_params=pltpu.CompilerParams(vmem_limit_bytes=16 * 2**20),
        cost_estimate=pl.CostEstimate(flops=1 << 28, bytes_accessed=4 << 20, transcendentals=0),
    )(place, *pieces)


def solution(mesh):
    grid = Mesh(mesh.devices.reshape(8, 8, 4, 2), ("y", "z", "x", "c"))
    tensor = ("z", "x", "c")
    in_specs = (
        P(tensor, None, None),
        P("y", tensor, None, None),
        P("y", tensor, None, None),
        P("y", None),
        P(tensor),
        P(tensor),
        P(tensor, None),
        P(tensor),
    )
    return jax.shard_map(
        on_device, mesh=grid, in_specs=in_specs, out_specs=P(tensor, None, None), check_vma=False
    )
```
